256 devices in a mesh: ctx: 64 (over x_lo, z, y), head: 4 (over x_hi, core).
Axes of the slice: x: 4 (x_hi: 2, x_lo: 2; x = x_hi * 2 + x_lo), y: 4, z: 8, core: 2. Of those that a mesh axis runs over, the one named last changes fastest.
Arguments:
- queries: bfloat16 [8192, 64, 576], P('ctx', 'head')
- compressed_kv: bfloat16 [8192, 576], P(('ctx', 'head')), may hold values from -4.5 to 4.5
- segment_ids: int32 [8192], P(('ctx', 'head')), may hold values from 0 to 11, never falling along the last dimension, each value on 1 to 2176 neighbouring positions
- value_up: bfloat16 [64, 512, 128], P('head'), may hold values from -0.25 to 0.25
Outputs:
- head_values: bfloat16 [8192, 8192], P('ctx', 'head')
The draws below stay inside these ranges and needn't reach their ends.
Inputs may be any that keep to these rules, and one draw needn't show every extreme that they name: `segment_ids`: ids never fall along the sequence and every document holds at most 2176 tokens; one holds exactly 2176.
All inputs are finite; a program needn't handle non-finite values.
Results may differ from the reference program's by a relative error of at most 0.0085.
Values may be sent and summed in bfloat16 or wider, within the bound.
A program may use at most 192 MiB of HBM per device.

```python
import math
import jax
import jax.numpy as jnp
import numpy as np
from jax import lax

H = 64
LATENT = 512
ROPE = 64
VDIM = 128
TOK_DEV = 128
TOKENS = 8192
DOC_MOST = 2176


def shared_rows(key):
    return jnp.clip(jax.random.normal(key, (TOKENS, LATENT + ROPE), jnp.float32), -4.5, 4.5)


def draw_compressed_kv(key, part):
    latent_rows = shared_rows(key)
    return latent_rows.astype(jnp.bfloat16)


def draw_queries(key, part):
    key = jax.random.fold_in(key, 2)
    first_key = jax.random.fold_in(key, 0)
    base_draw = jnp.clip(jax.random.normal(first_key, (TOKENS, H, LATENT + ROPE), jnp.float32), -4.5, 4.5)
    return base_draw.astype(jnp.bfloat16)


def level_of(rng, shape, cuts, low, high):
    level, own = 1.0, jax.random.fold_in(rng, 6)
    for axis_at, shards_of in cuts:
        heights = jnp.exp(jax.random.uniform(jax.random.fold_in(own, axis_at), (shards_of,), jnp.float32, low / len(cuts), high / len(cuts)))
        level = level * jnp.repeat(heights, shape[axis_at] // shards_of).reshape([-1 if axis == axis_at else 1 for axis in range(len(shape))])
    return level


def split_up(count, total, limit, lean):
    weights = [(1 << 20) // math.isqrt(rank ** lean) + 1 for rank in range(2, count + 1)]
    surplus, counts = total - limit - (count - 1), [1] * (count - 1)
    while surplus > 0:
        free = [i for i in range(count - 1) if counts[i] < limit]
        mass, remaining = sum([weights[i] for i in free]), surplus
        for i in free:
            more = min(limit - counts[i], max(1, remaining * weights[i] // mass), surplus)
            counts[i] = counts[i] + more
            surplus = surplus - more
    return np.array([limit] + counts)


def uneven_parts(stream_key, count, total, most, lean):
    if count == 2:
        one = jax.random.randint(stream_key, (), max(1, total - most), min(most, total - 1) + 1)
        return jnp.stack([one, total - one])
    sizes = jnp.asarray(split_up(count, total, most, lean), jnp.int32)
    couples = (count - 1) // 2
    source_of, receiver = sizes[1:1 + 2 * couples:2], sizes[2:2 + 2 * couples:2]
    slack = jnp.minimum(source_of - 1, most - receiver)
    moved = jax.random.randint(jax.random.fold_in(stream_key, 1), (couples,), 0, 1 << 20) % (slack + 1)
    sizes = sizes.at[1:1 + 2 * couples:2].set(source_of - moved).at[2:2 + 2 * couples:2].set(receiver + moved)
    return sizes[jax.random.permutation(jax.random.fold_in(stream_key, 2), count)]


def scatter_about(key, dims, deviation, most, shards=(), kind=jnp.bfloat16):
    entries = jax.random.normal(key, dims, jnp.float32) * deviation
    if len(shards) > 0:
        entries = level_of(key, dims, shards, -0.22, 0.18) * entries
    return jnp.clip(entries, min=-most, max=most).astype(kind)


def setup_inputs(seed: int = 0) -> dict:
    arg_keys = jax.random.split(jax.random.key(seed), 5)
    return {
        "queries": draw_queries(jax.random.fold_in(arg_keys[4], 71), 0),
        "compressed_kv": draw_compressed_kv(jax.random.fold_in(arg_keys[4], 71), 0),
        "segment_ids": jnp.searchsorted(jnp.cumsum(uneven_parts(arg_keys[2], 12, TOKENS, DOC_MOST, 2)), jnp.arange(TOKENS), side="right").astype(jnp.int32),
        "value_up": scatter_about(arg_keys[3], (H, LATENT, VDIM), LATENT ** -0.5, 0.25, ((0, 4),)),
    }


softmax_scale = 192.0 ** -0.5


def rotate_half(vectors, angles):
    half_width = vectors.shape[-1] // 2
    lower_half = vectors[..., :half_width]
    upper_half = vectors[..., half_width:]
    cosine = jnp.cos(angles)
    sine_part = jnp.sin(angles)
    return jnp.concatenate([lower_half * cosine - upper_half * sine_part, lower_half * sine_part + upper_half * cosine], axis=-1)


def angle_table(positions, width):
    inverse_freq = 10000.0 ** (-jnp.arange(width // 2, dtype=jnp.float32) / (width // 2))
    return positions.astype(jnp.float32)[:, None] * inverse_freq[None, :]


def reference(queries, compressed_kv, segment_ids, value_up):
    positions = jnp.arange(TOKENS, dtype=jnp.int32)
    angles = angle_table(positions, ROPE)
    key_rope = rotate_half(compressed_kv[:, LATENT:].astype(jnp.float32), angles).astype(jnp.bfloat16)
    key_full = jnp.concatenate([compressed_kv[:, :LATENT], key_rope], axis=1)
    query_rope = rotate_half(queries[:, :, LATENT:].astype(jnp.float32), angles[:, None, :]).astype(jnp.bfloat16)
    query_full = jnp.concatenate([queries[:, :, :LATENT], query_rope], axis=2)
    window = min(DOC_MOST + TOK_DEV, TOKENS)
    value_wide = value_up.astype(jnp.float32)

    def one_block(block_index):
        row_start = block_index * TOK_DEV
        key_start = jnp.maximum(row_start + TOK_DEV - window, 0).astype(jnp.int32)
        query_block = lax.dynamic_slice_in_dim(query_full, row_start, TOK_DEV, 0).astype(jnp.float32)
        key_block = lax.dynamic_slice_in_dim(key_full, key_start, window, 0).astype(jnp.float32)
        scores = jnp.einsum('thc,sc->ths', query_block, key_block) * softmax_scale
        query_pos = row_start + jnp.arange(TOK_DEV, dtype=jnp.int32)
        key_pos = key_start + jnp.arange(window, dtype=jnp.int32)
        query_seg = lax.dynamic_slice_in_dim(segment_ids, row_start, TOK_DEV, 0)
        key_seg = lax.dynamic_slice_in_dim(segment_ids, key_start, window, 0)
        allowed = (key_pos[None, :] <= query_pos[:, None]) & (key_seg[None, :] == query_seg[:, None])
        masked = jnp.where(allowed[:, None, :], scores, -jnp.inf)
        row_max = jnp.max(masked, axis=2, keepdims=True)
        raw_weights = jnp.exp(masked - row_max)
        denom_sum = jnp.sum(raw_weights, axis=2)
        rounded = lax.optimization_barrier(raw_weights.astype(jnp.bfloat16))
        weights = rounded.astype(jnp.float32)
        mixed_latent = jnp.einsum('ths,sc->thc', weights, key_block[:, :LATENT]) / denom_sum[:, :, None]
        mixed_round = lax.optimization_barrier(mixed_latent.astype(jnp.bfloat16))
        mixed_wide = mixed_round.astype(jnp.float32)
        return jnp.einsum('thc,hcv->thv', mixed_wide, value_wide).astype(jnp.bfloat16)

    outputs = lax.map(one_block, jnp.arange(TOKENS // TOK_DEV, dtype=jnp.int32))
    return outputs.reshape(TOKENS, H * VDIM)
```

```python
import functools
import math

import jax
import jax.numpy as jnp
import numpy as np
from jax import lax
from jax.experimental import pallas as pl
from jax.experimental.pallas import tpu as pltpu
from jax.sharding import PartitionSpec as P

MESH = pl.DeviceIdType.MESH
f32 = jnp.float32
bf16 = jnp.bfloat16

CTX = 64
TOK = 128
HEADS = 16
ROWS = TOK * HEADS
LATENT = 512
ROPE = 64
VDIM = 128
LANES = 128
QTR = TOK // 4
HALF = 2 * QTR
WIDTH = 640
BACK = 18
MASKED = -(2.0**100)
LOG_SCALE = (192.0**-0.5) * math.log2(math.e)
TILE = 512
GROUPS = ((0, 2), (2, 2), (4, 4), (8, 4), (12, 4), (16, 2))
QUARTERS_SENT = 35


def rope_table():
    freq = np.float32(10000.0) ** (-np.arange(ROPE // 2, dtype=np.float32) / np.float32(ROPE // 2))
    angle = (np.arange(CTX * TOK, dtype=np.float32)[:, None] * freq[None, :]).astype(np.float64)
    cos, sin = np.cos(angle), np.sin(angle)
    return np.concatenate([cos, cos, -sin, sin], axis=1).astype(np.float32)


def swap_halves(x):
    half = x.shape[-1] // 2
    return jnp.concatenate([x[..., half:], x[..., :half]], axis=-1)


def kernel(
    table_hbm, q_hbm, kv_ref, seg_ref, up_hbm, out_hbm,
    keys, q, q_rope, table, acc, top, total, s0, s1, p0, p1, f0, f1, up, out,
    in_sem, out_sem, send_sem, core_send_sem, z_sem, x_sem, row_sem, core_sem,
):
    c = lax.axis_index("ctx")
    h = lax.axis_index("head")
    x_hi, core = h // 2, h % 2
    y = c % 4
    mate_x = (1 - x_hi) * 2 + core
    mate_core = x_hi * 2 + (1 - core)
    quarter = pl.ds(pl.multiple_of(core * HALF + x_hi * QTR, QTR), QTR)
    half = pl.ds(pl.multiple_of(core * HALF, HALF), HALF)

    def ctx(by):
        return lax.rem(c + by + CTX, CTX)

    table_in = pltpu.make_async_copy(
        table_hbm.at[pl.ds(pl.multiple_of(c * TOK, TOK), TOK)], table, in_sem.at[0]
    )
    table_in.start()
    q_in = pltpu.make_async_copy(q_hbm.at[:, pl.ds(0, LATENT)], q.at[:, pl.ds(0, LATENT)], in_sem.at[1])
    q_rope_in = pltpu.make_async_copy(q_hbm.at[:, pl.ds(LATENT, ROPE)], q_rope, in_sem.at[2])
    q_rope_in.start()
    q_in.start()
    up_in = pltpu.make_async_copy(up_hbm, up, in_sem.at[3])

    barrier = pltpu.get_barrier_semaphore()

    def greet(to_ctx, to_head):
        pl.semaphore_signal(barrier, inc=1, device_id=(to_ctx, to_head), device_id_type=MESH)

    greet(c, mate_core)
    greet(c, mate_x)
    for k in range(1, 5):
        greet(ctx(-4 * k), h)
    row = 4 * (c // 4)
    for other in (core, 2 + core):
        greet(ctx(-1), other)
        for e in range(1, 4):
            greet(row + lax.rem(y - e + 4, 4), other)

    table_in.wait()
    own_rope = kv_ref[:, LATENT:].astype(f32)
    own_table = table[pl.ds(pl.multiple_of(h * QTR, QTR), QTR), :]
    own_rope = own_rope * own_table[:, :ROPE] + swap_halves(own_rope) * own_table[:, ROPE:]
    place = lax.broadcasted_iota(jnp.int32, (QTR, ROPE), 0)
    ids = jnp.zeros((QTR, ROPE), jnp.int32)
    for j in range(QTR):
        ids = jnp.where(place == j, seg_ref[j], ids)
    own_mark = jnp.where(lax.broadcasted_iota(jnp.int32, (QTR, ROPE), 1) == ids, 1.0, 0.0)
    keys[0, quarter, :LATENT] = kv_ref[:, :LATENT]
    keys[0, quarter, LATENT:] = jnp.concatenate([own_rope, own_mark], axis=1).astype(bf16)

    pl.semaphore_wait(barrier, 14)

    def send(k, d, to_ctx, to_head, sem):
        pltpu.make_async_remote_copy(
            src_ref=keys.at[4 * k, quarter],
            dst_ref=keys.at[d, quarter],
            send_sem=send_sem.at[0],
            recv_sem=sem,
            device_id=(to_ctx, to_head),
            device_id_type=MESH,
        ).start()

    def to_row(k, e, g, to_ctx):
        for other in (core, 2 + core):
            send(k, 4 * g + e, to_ctx, other, row_sem.at[4 * g + e])

    def pass_on(k):
        if k:
            pltpu.make_async_copy(keys.at[4 * k, quarter], keys.at[4 * k, quarter], z_sem.at[k]).wait()
        send(k, 4 * k, c, mate_x, x_sem.at[k])
        for e in (1, 3, 2):
            wrap = jnp.where(y + e >= 4, 1, 0)
            there = ctx(e - 4 * wrap)
            if e == 1 and k in (0, 4):
                to_row(k, e, k, ctx(1))
            if k == 0 and e > 1 or k == 1 and e == 1:
                pl.when(wrap == 0)(functools.partial(to_row, k, e, k, there))
            elif k == 4:
                pl.when(wrap == 1)(functools.partial(to_row, k, e, k - 1, there))
            elif k:
                to_row(k, e, k - wrap, there)

    def send_column(k):
        send(0, 4 * k, ctx(4 * k), h, z_sem.at[k])

    send_column(1)
    pass_on(0)
    for k in range(2, 5):
        send_column(k)
    up_in.start()

    def share(group):
        first, count = GROUPS[group]
        for d in range(first, first + count):
            if d % 4 == 0:
                pltpu.make_async_copy(keys.at[d, quarter], keys.at[d, quarter], x_sem.at[d // 4]).wait()
            else:
                pltpu.make_async_copy(keys.at[d, half], keys.at[d, half], row_sem.at[d]).wait()
        mine = keys.at[pl.ds(first, count), half]
        pltpu.make_async_remote_copy(
            src_ref=mine,
            dst_ref=mine,
            send_sem=core_send_sem.at[0],
            recv_sem=core_sem.at[group],
            device_id=(c, mate_core),
            device_id_type=MESH,
        ).start()

    def shared(group):
        first, count = GROUPS[group]
        theirs = keys.at[pl.ds(first, count), half]
        pltpu.make_async_copy(theirs, theirs, core_sem.at[group]).wait()

    q_rope_in.wait()
    for t in range(0, TOK, 32):
        part = q_rope[t * HEADS : (t + 32) * HEADS, :].astype(f32).reshape(32, HEADS, ROPE)
        cos = table[t : t + 32, :ROPE][:, None, :]
        sin = table[t : t + 32, ROPE:][:, None, :]
        part = part * cos + swap_halves(part) * sin
        q[t * HEADS : (t + 32) * HEADS, LATENT : LATENT + ROPE] = part.reshape(32 * HEADS, ROPE).astype(bf16)

    share(0)
    pass_on(1)
    q_in.wait()
    shared(0)

    for j in range(4):
        at = (j % 2) * HALF + (j // 2) * QTR
        mark = (keys[0, at : at + QTR, LATENT + ROPE :].astype(f32) - 1.0) * (-MASKED)
        mark = jnp.broadcast_to(mark[:, None, :], (QTR, HEADS, ROPE)).reshape(QTR * HEADS, ROPE)
        q[j * QTR * HEADS : (j + 1) * QTR * HEADS, LATENT + ROPE :] = mark.astype(bf16)

    tiles = ROWS // TILE
    work = [(g, t) for g in range(len(GROUPS)) for t in range(tiles)]
    scores, weights, factors = (s0, s1), (p0, p1), (f0, f1)

    def group_keys(group, columns):
        first, count = GROUPS[group]
        return keys[first : first + count, :, :columns].reshape(count * TOK, columns)

    def score(i):
        group, t = work[i]
        size = GROUPS[group][1] * TOK
        scores[i % 2][:, :size] = lax.dot_general(
            q[t * TILE : (t + 1) * TILE, :],
            group_keys(group, WIDTH),
            (((1,), (1,)), ((), ())),
            preferred_element_type=f32,
        )

    def weigh(i):
        group, t = work[i]
        count = GROUPS[group][1]
        at = slice(t * TILE, (t + 1) * TILE)
        parts = [scores[i % 2][:, j * TOK : (j + 1) * TOK] for j in range(count)]
        if group == 0:
            lane = lax.broadcasted_iota(jnp.int32, (TILE, TOK), 1)
            key_at = (lane // QTR % 2) * HALF + (lane // HALF) * QTR + lane % QTR
            query_at = lax.broadcasted_iota(jnp.int32, (TILE, TOK), 0) // HEADS + t * (TILE // HEADS)
            parts[0] = jnp.where(key_at <= query_at, parts[0], MASKED)
        high = functools.reduce(jnp.maximum, parts)
        high = jnp.max(high, axis=1, keepdims=True)
        if group == 0:
            high = jnp.broadcast_to(high, (TILE, TOK))
        else:
            before = top[at, :]
            high = jnp.maximum(before, high)
        shift = high * LOG_SCALE
        added = None
        for j in range(count):
            raw = jnp.exp2(parts[j] * LOG_SCALE - shift)
            weights[i % 2][:, j * TOK : (j + 1) * TOK] = raw.astype(bf16)
            added = raw if added is None else added + raw
        top[at, :] = high
        if group == 0:
            total[at, :] = added
        else:
            factor = jnp.exp2(before * LOG_SCALE - shift)
            factors[i % 2][...] = factor
            total[at, :] = total[at, :] * factor + added

    def mix(i):
        group, t = work[i]
        at = slice(t * TILE, (t + 1) * TILE)
        size = GROUPS[group][1] * TOK
        mixed = jnp.dot(weights[i % 2][:, :size], group_keys(group, LATENT), preferred_element_type=f32)
        for j in range(LATENT // LANES):
            part = mixed[:, j * LANES : (j + 1) * LANES]
            if group == 0:
                acc[j, at, :] = part
            else:
                acc[j, at, :] = acc[j, at, :] * factors[i % 2][...] + part

    before_step = {
        0: [lambda: pass_on(2)],
        1: [lambda: share(1)],
        2: [lambda: shared(1), lambda: pass_on(3)],
        5: [lambda: share(2)],
        6: [lambda: shared(2), lambda: pass_on(4)],
        9: [lambda: share(3)],
        10: [lambda: shared(3)],
        13: [lambda: share(4)],
        14: [lambda: shared(4)],
        17: [lambda: share(5)],
        18: [lambda: shared(5)],
    }
    score(0)
    score(1)
    weigh(0)
    for i in range(len(work)):
        for event in before_step.get(i, ()):
            event()
        mix(i)
        if i + 1 < len(work):
            weigh(i + 1)
        if i + 2 < len(work):
            score(i + 2)

    up_in.wait()
    per_copy = 4
    copies = []
    for head in range(HEADS):
        rows = pl.ds(head, TOK, stride=HEADS)
        share_of = 1.0 / jnp.sum(total[rows, :], axis=1, keepdims=True)
        mixed_latent = jnp.concatenate(
            [(acc[j, rows, :] * share_of).astype(bf16) for j in range(LATENT // LANES)], axis=1
        )
        out[:, head * VDIM : (head + 1) * VDIM] = jnp.dot(
            mixed_latent, up[head], preferred_element_type=f32
        ).astype(bf16)
        if head % per_copy == per_copy - 1:
            done = pl.ds((head + 1 - per_copy) * VDIM, per_copy * VDIM)
            copies.append(pltpu.make_async_copy(out.at[:, done], out_hbm.at[:, done], out_sem.at[head // per_copy]))
            copies[-1].start()
    everything = q.at[pl.ds(0, QUARTERS_SENT * QTR)]
    pltpu.make_async_copy(everything, everything, send_sem.at[0]).wait()
    everything = q.at[pl.ds(0, BACK * HALF)]
    pltpu.make_async_copy(everything, everything, core_send_sem.at[0]).wait()
    for copy in copies:
        copy.wait()


def local(queries, compressed_kv, segment_ids, value_up):
    any_space = pl.BlockSpec(memory_space=pl.ANY)
    return pl.pallas_call(
        kernel,
        out_shape=jax.ShapeDtypeStruct((TOK, HEADS * VDIM), bf16),
        in_specs=[
            any_space,
            any_space,
            pl.BlockSpec(memory_space=pltpu.VMEM),
            pl.BlockSpec(memory_space=pltpu.SMEM),
            any_space,
        ],
        out_specs=any_space,
        scratch_shapes=[
            pltpu.VMEM((BACK, TOK, WIDTH), bf16),
            pltpu.VMEM((ROWS, WIDTH), bf16),
            pltpu.VMEM((ROWS, ROPE), bf16),
            pltpu.VMEM((TOK, 2 * ROPE), f32),
            pltpu.VMEM((LATENT // LANES, ROWS, LANES), f32),
            pltpu.VMEM((ROWS, TOK), f32),
            pltpu.VMEM((ROWS, TOK), f32),
            pltpu.VMEM((TILE, 4 * TOK), f32),
            pltpu.VMEM((TILE, 4 * TOK), f32),
            pltpu.VMEM((TILE, 4 * TOK), bf16),
            pltpu.VMEM((TILE, 4 * TOK), bf16),
            pltpu.VMEM((TILE, TOK), f32),
            pltpu.VMEM((TILE, TOK), f32),
            pltpu.VMEM((HEADS, LATENT, VDIM), bf16),
            pltpu.VMEM((TOK, HEADS * VDIM), bf16),
            pltpu.SemaphoreType.DMA((4,)),
            pltpu.SemaphoreType.DMA((4,)),
            pltpu.SemaphoreType.DMA((1,)),
            pltpu.SemaphoreType.DMA((1,)),
            pltpu.SemaphoreType.DMA((5,)),
            pltpu.SemaphoreType.DMA((5,)),
            pltpu.SemaphoreType.DMA((BACK,)),
            pltpu.SemaphoreType.DMA((len(GROUPS),)),
        ],
        compiler_params=pltpu.CompilerParams(
            collective_id=0, has_side_effects=True, vmem_limit_bytes=44 << 20
        ),
        name="latent_attention",
    )(
        jnp.asarray(rope_table()),
        queries.reshape(ROWS, LATENT + ROPE),
        compressed_kv,
        segment_ids,
        value_up,
    )


def solution(mesh):
    in_specs = (
        P("ctx", "head", None),
        P(("ctx", "head"), None),
        P(("ctx", "head")),
        P("head", None, None),
    )
    return jax.shard_map(
        local, mesh=mesh, in_specs=in_specs, out_specs=P("ctx", "head"), check_vma=False
    )
```

```python
import functools
import math

import jax
import jax.numpy as jnp
import numpy as np
from jax import lax
from jax.experimental import pallas as pl
from jax.experimental.pallas import tpu as pltpu
from jax.sharding import PartitionSpec as P

MESH = pl.DeviceIdType.MESH
f32 = jnp.float32
bf16 = jnp.bfloat16

CTX = 64
TOK = 128
HEADS = 16
ROWS = TOK * HEADS
LATENT = 512
ROPE = 64
VDIM = 128
LANES = 128
QTR = TOK // 4
HALF = 2 * QTR
WIDTH = 640
BACK = 18
MASKED = -(2.0**100)
LOG_SCALE = (192.0**-0.5) * math.log2(math.e)
TILE = 512
GROUPS = ((0, 2), (2, 2), (4, 4), (8, 4), (12, 4), (16, 2))
HALF_ROPE = ROPE // 2
SENDS = 57
BY_MATE = ()
FROM_BOTH = (0, 1, 2, 3, 4)


def rope_table():
    freq = np.float32(10000.0) ** (-np.arange(HALF_ROPE, dtype=np.float32) / np.float32(HALF_ROPE))
    position = np.arange(CTX * TOK, dtype=np.float32).reshape(CTX, 1, TOK)
    angle = (position * freq[None, :, None]).astype(np.float64)
    return np.concatenate([np.cos(angle), np.sin(angle)], axis=1).astype(np.float32)


def kernel(
    table_hbm, q_hbm, kv_hbm, seg_hbm, up_hbm, out_hbm,
    keys, q, q_flat, kv, seg, table, table_rows, acc, top, total, s0, s1, p0, p1, f0, f1, up, out,
    in_sem, out_sem, send_sem, core_send_sem, z_sem, x_sem, row_sem, core_sem,
):
    c = lax.axis_index("ctx")
    h = lax.axis_index("head")
    x_hi, core = h // 2, h % 2
    y = c % 4
    mate_x = (1 - x_hi) * 2 + core
    mate_core = x_hi * 2 + (1 - core)
    quarter = pl.ds(pl.multiple_of(core * HALF + x_hi * QTR, QTR), QTR)
    half = pl.ds(pl.multiple_of(core * HALF, HALF), HALF)

    kv_in = pltpu.make_async_copy(kv_hbm, kv, in_sem.at[0])
    seg_in = pltpu.make_async_copy(seg_hbm, seg, in_sem.at[1])
    table_in = pltpu.make_async_copy(table_hbm.at[c], table, in_sem.at[2])
    q_in = pltpu.make_async_copy(q_hbm, q_flat, in_sem.at[3])
    up_in = pltpu.make_async_copy(up_hbm, up, in_sem.at[4])
    for copy in (kv_in, seg_in, table_in, q_in):
        copy.start()

    barrier = pltpu.get_barrier_semaphore()

    def greet(to_ctx, to_head):
        pl.semaphore_signal(barrier, inc=1, device_id=(to_ctx, to_head), device_id_type=MESH)

    row = c - y
    greet(c, mate_core)
    greet(c, mate_x)
    for other in (core, 2 + core):
        for e in range(1, 4):
            greet(row + lax.rem(y - e + 4, 4), other)
        pl.when(c >= 1)(functools.partial(greet, c - 1, other))
    for k in (1, 2):
        pl.when(c >= 4 * k)(functools.partial(greet, c - 4 * k, h))
    expected = 8 + 2 * jnp.where(c + 1 < CTX, 1, 0) + jnp.where(c + 4 < CTX, 1, 0) + jnp.where(c + 8 < CTX, 1, 0)

    @pl.when(c < BACK - 1)
    def _():
        for d in range(1, BACK):

            @pl.when(d > c)
            def _():
                keys[d, half, :LATENT] = jnp.zeros((HALF, LATENT), bf16)
                lane = lax.broadcasted_iota(jnp.int32, (HALF, LANES), 1)
                keys[d, half, LATENT:] = jnp.where(lane < ROPE, 0.0, 1.0).astype(bf16)

    table_in.wait()
    table_rows[...] = table[...].T
    kv_in.wait()
    own_table = table_rows[pl.ds(pl.multiple_of(h * QTR, QTR), QTR), :]
    own_cos, own_sin = own_table[:, :HALF_ROPE], own_table[:, HALF_ROPE:]
    own_rope = kv[:, LATENT:].astype(f32)
    low, high = own_rope[:, :HALF_ROPE], own_rope[:, HALF_ROPE:]
    seg_in.wait()
    place = lax.broadcasted_iota(jnp.int32, (QTR, ROPE), 0)
    ids = jnp.zeros((QTR, ROPE), jnp.int32)
    for j in range(QTR):
        ids = jnp.where(place == j, seg[j], ids)
    own_mark = jnp.where(lax.broadcasted_iota(jnp.int32, (QTR, ROPE), 1) == ids, 1.0, 0.0)
    keys[0, quarter, :LATENT] = kv[:, :LATENT]
    keys[0, quarter, LATENT:] = jnp.concatenate(
        [low * own_cos - high * own_sin, low * own_sin + high * own_cos, own_mark], axis=1
    ).astype(bf16)

    pl.semaphore_wait(barrier, expected)

    sent = []

    def send(src, dst, to_ctx, to_head, sem, when):
        copy = pltpu.make_async_remote_copy(
            src_ref=src,
            dst_ref=dst,
            send_sem=send_sem.at[len(sent)],
            recv_sem=sem,
            device_id=(to_ctx, to_head),
            device_id_type=MESH,
        )
        sent.append((when, copy))
        pl.when(when)(copy.start)

    def arrived(view, sem, when):
        pl.when(when)(pltpu.make_async_copy(view, view, sem).wait)

    def column(k, hops):
        to = c + 4 * hops
        there = keys.at[4 * (k + hops), quarter]
        send(keys.at[4 * k, quarter], there, to, h, z_sem.at[k + hops], (c >= 4 * k) & (to < CTX))

    def across(d):
        send(keys.at[d, quarter], keys.at[d, quarter], c, mate_x, x_sem.at[d], c >= d)

    def relay(k, whole):
        for wrapped in (1, 0):
            for e in (1, 2, 3):
                d = 4 * (k - wrapped) + e
                to = c + e - 4 * wrapped
                if d < 0 or d >= BACK or (d == 1 and wrapped) or whole == (d in BY_MATE or k in FROM_BOTH):
                    continue
                when = (y + e >= 4) == (wrapped == 1)
                if d in (1, 17):
                    when = to < CTX
                when = when & (c >= 4 * k)
                if d in BY_MATE:
                    send(keys.at[4 * k, quarter], keys.at[d, quarter], to, h, row_sem.at[d], when)
                elif whole:
                    send(keys.at[4 * k, half], keys.at[d, half], to, h, row_sem.at[d], when)
                else:
                    for other in (core, 2 + core):
                        send(keys.at[4 * k, quarter], keys.at[d, quarter], to, other, row_sem.at[d], when)

    def column_in(k):
        if k == 0:
            column(0, 1)
            column(0, 2)
        else:
            arrived(keys.at[4 * k, quarter], z_sem.at[k], c >= 4 * k)
        if k == 2:
            column(2, 1)
            column(2, 2)
        across(4 * k)
        relay(k, False)

    def column_whole(k):
        arrived(keys.at[4 * k, quarter], x_sem.at[4 * k], c >= 4 * k)
        relay(k, True)

    def row_in(d):
        arrived(keys.at[d, quarter], row_sem.at[d], c >= d)
        across(d)

    def share(group):
        first, count = GROUPS[group]
        for d in range(first, first + count):
            if d in BY_MATE:
                arrived(keys.at[d, quarter], x_sem.at[d], c >= d)
            elif d % 4:
                arrived(keys.at[d, half], row_sem.at[d], c >= d)
        mine = keys.at[pl.ds(first, count), half]
        pltpu.make_async_remote_copy(
            src_ref=mine,
            dst_ref=mine,
            send_sem=core_send_sem.at[0],
            recv_sem=core_sem.at[group],
            device_id=(c, mate_core),
            device_id_type=MESH,
        ).start()

    def shared(group):
        first, count = GROUPS[group]
        theirs = keys.at[pl.ds(first, count), half]
        pltpu.make_async_copy(theirs, theirs, core_sem.at[group]).wait()

    column_in(0)
    up_in.start()

    q_in.wait()
    cos, sin = table[:HALF_ROPE, :], table[HALF_ROPE:, :]
    for head in range(HEADS):
        at = slice(head * TOK, (head + 1) * TOK)
        for j in range(LATENT // LANES):
            q[at, j * LANES : (j + 1) * LANES] = q_flat[head, j * LANES : (j + 1) * LANES, :].T
        low = q_flat[head, LATENT : LATENT + HALF_ROPE, :].astype(f32)
        high = q_flat[head, LATENT + HALF_ROPE :, :].astype(f32)
        turned = jnp.concatenate([low * cos - high * sin, low * sin + high * cos], axis=0)
        q[at, LATENT : LATENT + ROPE] = turned.T.astype(bf16)

    column_in(1)
    column_whole(0)
    share(0)
    column_in(2)
    shared(0)

    for j in range(4):
        at = (j % 2) * HALF + (j // 2) * QTR
        mark = ((keys[0, at : at + QTR, LATENT + ROPE :].astype(f32) - 1.0) * (-MASKED)).astype(bf16)
        for head in range(HEADS):
            q[head * TOK + j * QTR : head * TOK + (j + 1) * QTR, LATENT + ROPE :] = mark

    tiles = ROWS // TILE
    work = [(g, t) for g in range(len(GROUPS)) for t in range(tiles)]
    scores, weights, factors = (s0, s1), (p0, p1), (f0, f1)

    def group_keys(group, columns):
        first, count = GROUPS[group]
        return keys[first : first + count, :, :columns].reshape(count * TOK, columns)

    def score(i):
        group, t = work[i]
        size = GROUPS[group][1] * TOK
        scores[i % 2][:, :size] = lax.dot_general(
            q[t * TILE : (t + 1) * TILE, :],
            group_keys(group, WIDTH),
            (((1,), (1,)), ((), ())),
            preferred_element_type=f32,
        )

    def weigh(i):
        group, t = work[i]
        count = GROUPS[group][1]
        at = slice(t * TILE, (t + 1) * TILE)
        parts = [scores[i % 2][:, j * TOK : (j + 1) * TOK] for j in range(count)]
        if group == 0:
            lane = lax.broadcasted_iota(jnp.int32, (TILE, TOK), 1)
            key_at = (lane // QTR % 2) * HALF + (lane // HALF) * QTR + lane % QTR
            query_at = lax.broadcasted_iota(jnp.int32, (TILE, TOK), 0) % TOK
            parts[0] = jnp.where(key_at <= query_at, parts[0], MASKED)
        high = functools.reduce(jnp.maximum, parts)
        high = jnp.max(high, axis=1, keepdims=True)
        if group == 0:
            high = jnp.broadcast_to(high, (TILE, TOK))
        else:
            before = top[at, :]
            high = jnp.maximum(before, high)
        shift = high * LOG_SCALE
        added = None
        for j in range(count):
            raw = jnp.exp2(parts[j] * LOG_SCALE - shift)
            weights[i % 2][:, j * TOK : (j + 1) * TOK] = raw.astype(bf16)
            added = raw if added is None else added + raw
        top[at, :] = high
        if group == 0:
            total[at, :] = added
        else:
            factor = jnp.exp2(before * LOG_SCALE - shift)
            factors[i % 2][...] = factor
            total[at, :] = total[at, :] * factor + added

    def mix(i):
        group, t = work[i]
        at = slice(t * TILE, (t + 1) * TILE)
        size = GROUPS[group][1] * TOK
        mixed = jnp.dot(weights[i % 2][:, :size], group_keys(group, LATENT), preferred_element_type=f32)
        if group == 0:
            acc[at, :] = mixed
        else:
            factor = factors[i % 2][...]
            acc[at, :] = acc[at, :] * jnp.concatenate([factor] * (LATENT // LANES), axis=1) + mixed

    copies = []

    def finish(t):
        for head in range(t * TILE // TOK, (t + 1) * TILE // TOK):
            at = slice(head * TOK, (head + 1) * TOK)
            scale = 1.0 / jnp.sum(total[at, :], axis=1, keepdims=True)
            out[:, head * VDIM : (head + 1) * VDIM] = jnp.dot(
                (acc[at, :] * scale).astype(bf16), up[head], preferred_element_type=f32
            ).astype(bf16)
        done = pl.ds(t * TILE, TILE)
        copies.append(pltpu.make_async_copy(out.at[:, done], out_hbm.at[:, done], out_sem.at[t]))
        copies[-1].start()

    before_step = {
        0: [lambda: column_in(3)],
        1: [lambda: column_whole(1), lambda: share(1)],
        2: [lambda: column_in(4), lambda: shared(1)],
        4: [lambda: share(2)],
        6: [lambda: shared(2)],
        8: [lambda: column_whole(2), lambda: share(3)],
        10: [lambda: shared(3)],
        12: [lambda: column_whole(3), lambda: share(4)],
        14: [lambda: shared(4)],
        16: [lambda: column_whole(4), lambda: share(5)],
        18: [lambda: shared(5)],
    }
    score(0)
    score(1)
    weigh(0)
    for i in range(len(work)):
        for event in before_step.get(i, ()):
            event()
        if i == len(work) - tiles:
            up_in.wait()
        mix(i)
        if i + 1 < len(work):
            weigh(i + 1)
        if i + 2 < len(work):
            score(i + 2)
        if i >= len(work) - tiles:
            finish(i - (len(work) - tiles))

    assert len(sent) == SENDS, len(sent)
    for when, copy in sent:
        pl.when(when)(copy.wait_send)
    everything = q.at[pl.ds(0, BACK * HALF)]
    pltpu.make_async_copy(everything, everything, core_send_sem.at[0]).wait()
    for copy in copies:
        copy.wait()


def local(queries, compressed_kv, segment_ids, value_up):
    any_space = pl.BlockSpec(memory_space=pl.ANY)
    return pl.pallas_call(
        kernel,
        out_shape=jax.ShapeDtypeStruct((TOK, HEADS * VDIM), bf16),
        in_specs=[any_space] * 5,
        out_specs=any_space,
        scratch_shapes=[
            pltpu.VMEM((BACK, TOK, WIDTH), bf16),
            pltpu.VMEM((ROWS, WIDTH), bf16),
            pltpu.VMEM((HEADS, LATENT + ROPE, TOK), bf16),
            pltpu.VMEM((QTR, LATENT + ROPE), bf16),
            pltpu.SMEM((QTR,), jnp.int32),
            pltpu.VMEM((ROPE, TOK), f32),
            pltpu.VMEM((TOK, ROPE), f32),
            pltpu.VMEM((ROWS, LATENT), f32),
            pltpu.VMEM((ROWS, TOK), f32),
            pltpu.VMEM((ROWS, TOK), f32),
            pltpu.VMEM((TILE, 4 * TOK), f32),
            pltpu.VMEM((TILE, 4 * TOK), f32),
            pltpu.VMEM((TILE, 4 * TOK), bf16),
            pltpu.VMEM((TILE, 4 * TOK), bf16),
            pltpu.VMEM((TILE, TOK), f32),
            pltpu.VMEM((TILE, TOK), f32),
            pltpu.VMEM((HEADS, LATENT, VDIM), bf16),
            pltpu.VMEM((TOK, HEADS * VDIM), bf16),
            pltpu.SemaphoreType.DMA((5,)),
            pltpu.SemaphoreType.DMA((4,)),
            pltpu.SemaphoreType.DMA((SENDS,)),
            pltpu.SemaphoreType.DMA((1,)),
            pltpu.SemaphoreType.DMA((5,)),
            pltpu.SemaphoreType.DMA((BACK,)),
            pltpu.SemaphoreType.DMA((BACK,)),
            pltpu.SemaphoreType.DMA((len(GROUPS),)),
        ],
        compiler_params=pltpu.CompilerParams(
            collective_id=0, has_side_effects=True, vmem_limit_bytes=62 << 20
        ),
        name="latent_attention",
    )(
        jnp.asarray(rope_table()),
        jnp.transpose(queries, (1, 2, 0)),
        compressed_kv,
        segment_ids,
        value_up,
    )


def solution(mesh):
    in_specs = (
        P("ctx", "head", None),
        P(("ctx", "head"), None),
        P(("ctx", "head")),
        P("head", None, None),
    )
    return jax.shard_map(
        local, mesh=mesh, in_specs=in_specs, out_specs=P("ctx", "head"), check_vma=False
    )
```

```python
import functools
import math

import jax
import jax.numpy as jnp
import numpy as np
from jax import lax
from jax.experimental import pallas as pl
from jax.experimental.pallas import tpu as pltpu
from jax.sharding import PartitionSpec as P

MESH = pl.DeviceIdType.MESH
f32 = jnp.float32
bf16 = jnp.bfloat16

CTX = 64
TOK = 128
HEADS = 16
ROWS = TOK * HEADS
LATENT = 512
ROPE = 64
VDIM = 128
LANES = 128
QTR = TOK // 4
HALF = 2 * QTR
WIDTH = 640
BACK = 18
MASKED = -(2.0**100)
LOG_SCALE = (192.0**-0.5) * math.log2(math.e)
TILE = 512
GROUPS = ((0, 2), (2, 2), (4, 4), (8, 4), (12, 4), (16, 2))
HALF_ROPE = ROPE // 2
SENDS = 57
BY_MATE = ()
FROM_BOTH = (0, 1, 2, 3, 4)


def rope_table():
    freq = np.float32(10000.0) ** (-np.arange(HALF_ROPE, dtype=np.float32) / np.float32(HALF_ROPE))
    position = np.arange(CTX * TOK, dtype=np.float32).reshape(CTX, 1, TOK)
    angle = (position * freq[None, :, None]).astype(np.float64)
    return np.concatenate([np.cos(angle), np.sin(angle)], axis=1).astype(np.float32)


def kernel(
    table_hbm, q_hbm, kv_hbm, seg_hbm, up_hbm, out_hbm,
    keys, q, q_flat, kv, seg, table, table_rows, acc, top, total, s0, s1, p0, p1, f0, f1, up, out,
    in_sem, out_sem, send_sem, core_send_sem, z_sem, x_sem, row_sem, core_sem,
):
    c = lax.axis_index("ctx")
    h = lax.axis_index("head")
    x_hi, core = h // 2, h % 2
    y = c % 4
    mate_x = (1 - x_hi) * 2 + core
    mate_core = x_hi * 2 + (1 - core)
    quarter = pl.ds(pl.multiple_of(core * HALF + x_hi * QTR, QTR), QTR)
    half = pl.ds(pl.multiple_of(core * HALF, HALF), HALF)

    kv_in = pltpu.make_async_copy(kv_hbm, kv, in_sem.at[0])
    seg_in = pltpu.make_async_copy(seg_hbm, seg, in_sem.at[1])
    table_in = pltpu.make_async_copy(table_hbm.at[c], table, in_sem.at[2])
    q_in = pltpu.make_async_copy(q_hbm, q_flat, in_sem.at[3])
    up_in = pltpu.make_async_copy(up_hbm, up, in_sem.at[4])
    for copy in (kv_in, seg_in, table_in, q_in):
        copy.start()

    barrier = pltpu.get_barrier_semaphore()

    def greet(to_ctx, to_head):
        pl.semaphore_signal(barrier, inc=1, device_id=(to_ctx, to_head), device_id_type=MESH)

    row = c - y
    greet(c, mate_core)
    greet(c, mate_x)
    for other in (core, 2 + core):
        for e in range(1, 4):
            greet(row + lax.rem(y - e + 4, 4), other)
        pl.when(c >= 1)(functools.partial(greet, c - 1, other))
    for k in (1, 2):
        pl.when(c >= 4 * k)(functools.partial(greet, c - 4 * k, h))
    expected = 8 + 2 * jnp.where(c + 1 < CTX, 1, 0) + jnp.where(c + 4 < CTX, 1, 0) + jnp.where(c + 8 < CTX, 1, 0)

    @pl.when(c < BACK - 1)
    def _():
        for d in range(1, BACK):

            @pl.when(d > c)
            def _():
                keys[d, half, :LATENT] = jnp.zeros((HALF, LATENT), bf16)
                lane = lax.broadcasted_iota(jnp.int32, (HALF, LANES), 1)
                keys[d, half, LATENT:] = jnp.where(lane < ROPE, 0.0, 1.0).astype(bf16)

    kv_in.wait()
    keys[0, quarter, :LATENT] = kv[:, :LATENT]
    seg_in.wait()
    place = lax.broadcasted_iota(jnp.int32, (QTR, ROPE), 0)
    ids = jnp.zeros((QTR, ROPE), jnp.int32)
    for j in range(QTR):
        ids = jnp.where(place == j, seg[j], ids)
    own_mark = jnp.where(lax.broadcasted_iota(jnp.int32, (QTR, ROPE), 1) == ids, 1.0, 0.0)
    table_in.wait()
    table_rows[...] = table[...].T
    own_table = table_rows[pl.ds(pl.multiple_of(h * QTR, QTR), QTR), :]
    own_cos, own_sin = own_table[:, :HALF_ROPE], own_table[:, HALF_ROPE:]
    own_rope = kv[:, LATENT:].astype(f32)
    low, high = own_rope[:, :HALF_ROPE], own_rope[:, HALF_ROPE:]
    keys[0, quarter, LATENT:] = jnp.concatenate(
        [low * own_cos - high * own_sin, low * own_sin + high * own_cos, own_mark], axis=1
    ).astype(bf16)

    pl.semaphore_wait(barrier, expected)

    sent = []

    def send(src, dst, to_ctx, to_head, sem, when):
        copy = pltpu.make_async_remote_copy(
            src_ref=src,
            dst_ref=dst,
            send_sem=send_sem.at[len(sent)],
            recv_sem=sem,
            device_id=(to_ctx, to_head),
            device_id_type=MESH,
        )
        sent.append((when, copy))
        pl.when(when)(copy.start)

    def arrived(view, sem, when):
        pl.when(when)(pltpu.make_async_copy(view, view, sem).wait)

    def column(k, hops):
        to = c + 4 * hops
        there = keys.at[4 * (k + hops), quarter]
        send(keys.at[4 * k, quarter], there, to, h, z_sem.at[k + hops], (c >= 4 * k) & (to < CTX))

    def across(d):
        send(keys.at[d, quarter], keys.at[d, quarter], c, mate_x, x_sem.at[d], c >= d)

    def relay(k, whole):
        for wrapped in (1, 0):
            for e in (1, 2, 3):
                d = 4 * (k - wrapped) + e
                to = c + e - 4 * wrapped
                if d < 0 or d >= BACK or (d == 1 and wrapped) or whole == (d in BY_MATE or k in FROM_BOTH):
                    continue
                when = (y + e >= 4) == (wrapped == 1)
                if d in (1, 17):
                    when = to < CTX
                when = when & (c >= 4 * k)
                if d in BY_MATE:
                    send(keys.at[4 * k, quarter], keys.at[d, quarter], to, h, row_sem.at[d], when)
                elif whole:
                    send(keys.at[4 * k, half], keys.at[d, half], to, h, row_sem.at[d], when)
                else:
                    for other in (core, 2 + core):
                        send(keys.at[4 * k, quarter], keys.at[d, quarter], to, other, row_sem.at[d], when)

    def column_in(k):
        if k == 0:
            column(0, 1)
            column(0, 2)
        else:
            arrived(keys.at[4 * k, quarter], z_sem.at[k], c >= 4 * k)
        if k == 2:
            column(2, 1)
            column(2, 2)
        across(4 * k)
        relay(k, False)

    def column_whole(k):
        arrived(keys.at[4 * k, quarter], x_sem.at[4 * k], c >= 4 * k)
        relay(k, True)

    def row_in(d):
        arrived(keys.at[d, quarter], row_sem.at[d], c >= d)
        across(d)

    def share(group):
        first, count = GROUPS[group]
        for d in range(first, first + count):
            if d in BY_MATE:
                arrived(keys.at[d, quarter], x_sem.at[d], c >= d)
            elif d % 4:
                arrived(keys.at[d, half], row_sem.at[d], c >= d)
        mine = keys.at[pl.ds(first, count), half]
        pltpu.make_async_remote_copy(
            src_ref=mine,
            dst_ref=mine,
            send_sem=core_send_sem.at[0],
            recv_sem=core_sem.at[group],
            device_id=(c, mate_core),
            device_id_type=MESH,
        ).start()

    def shared(group):
        first, count = GROUPS[group]
        theirs = keys.at[pl.ds(first, count), half]
        pltpu.make_async_copy(theirs, theirs, core_sem.at[group]).wait()

    column_in(0)
    up_in.start()

    q_in.wait()
    cos, sin = table[:HALF_ROPE, :], table[HALF_ROPE:, :]
    for head in range(HEADS):
        at = slice(head * TOK, (head + 1) * TOK)
        for j in range(LATENT // LANES):
            q[at, j * LANES : (j + 1) * LANES] = q_flat[head, j * LANES : (j + 1) * LANES, :].T
        low = q_flat[head, LATENT : LATENT + HALF_ROPE, :].astype(f32)
        high = q_flat[head, LATENT + HALF_ROPE :, :].astype(f32)
        turned = jnp.concatenate([low * cos - high * sin, low * sin + high * cos], axis=0)
        q[at, LATENT : LATENT + ROPE] = turned.T.astype(bf16)

    column_in(1)
    column_whole(0)
    share(0)
    column_in(2)
    shared(0)

    for j in range(4):
        at = (j % 2) * HALF + (j // 2) * QTR
        mark = ((keys[0, at : at + QTR, LATENT + ROPE :].astype(f32) - 1.0) * (-MASKED)).astype(bf16)
        for head in range(HEADS):
            q[head * TOK + j * QTR : head * TOK + (j + 1) * QTR, LATENT + ROPE :] = mark

    tiles = ROWS // TILE
    work = [(g, t) for g in range(len(GROUPS)) for t in range(tiles)]
    scores, weights, factors = (s0, s1), (p0, p1), (f0, f1)

    def group_keys(group, columns):
        first, count = GROUPS[group]
        return keys[first : first + count, :, :columns].reshape(count * TOK, columns)

    def score(i):
        group, t = work[i]
        size = GROUPS[group][1] * TOK
        scores[i % 2][:, :size] = lax.dot_general(
            q[t * TILE : (t + 1) * TILE, :],
            group_keys(group, WIDTH),
            (((1,), (1,)), ((), ())),
            preferred_element_type=f32,
        )

    def weigh(i):
        group, t = work[i]
        count = GROUPS[group][1]
        at = slice(t * TILE, (t + 1) * TILE)
        parts = [scores[i % 2][:, j * TOK : (j + 1) * TOK] for j in range(count)]
        if group == 0:
            lane = lax.broadcasted_iota(jnp.int32, (TILE, TOK), 1)
            key_at = (lane // QTR % 2) * HALF + (lane // HALF) * QTR + lane % QTR
            query_at = lax.broadcasted_iota(jnp.int32, (TILE, TOK), 0) % TOK
            parts[0] = jnp.where(key_at <= query_at, parts[0], MASKED)
        high = functools.reduce(jnp.maximum, parts)
        high = jnp.max(high, axis=1, keepdims=True)
        if group == 0:
            high = jnp.broadcast_to(high, (TILE, TOK))
        else:
            before = top[at, :]
            high = jnp.maximum(before, high)
        shift = high * LOG_SCALE
        added = None
        for j in range(count):
            raw = jnp.exp2(parts[j] * LOG_SCALE - shift)
            weights[i % 2][:, j * TOK : (j + 1) * TOK] = raw.astype(bf16)
            added = raw if added is None else added + raw
        top[at, :] = high
        if group == 0:
            total[at, :] = added
        else:
            factor = jnp.exp2(before * LOG_SCALE - shift)
            factors[i % 2][...] = factor
            total[at, :] = total[at, :] * factor + added

    def mix(i):
        group, t = work[i]
        at = slice(t * TILE, (t + 1) * TILE)
        size = GROUPS[group][1] * TOK
        mixed = jnp.dot(weights[i % 2][:, :size], group_keys(group, LATENT), preferred_element_type=f32)
        if group == 0:
            acc[at, :] = mixed
        else:
            factor = factors[i % 2][...]
            acc[at, :] = acc[at, :] * jnp.concatenate([factor] * (LATENT // LANES), axis=1) + mixed

    copies = []

    def finish(t):
        for head in range(t * TILE // TOK, (t + 1) * TILE // TOK):
            at = slice(head * TOK, (head + 1) * TOK)
            scale = 1.0 / jnp.sum(total[at, :], axis=1, keepdims=True)
            out[:, head * VDIM : (head + 1) * VDIM] = jnp.dot(
                (acc[at, :] * scale).astype(bf16), up[head], preferred_element_type=f32
            ).astype(bf16)
        done = pl.ds(t * TILE, TILE)
        copies.append(pltpu.make_async_copy(out.at[:, done], out_hbm.at[:, done], out_sem.at[t]))
        copies[-1].start()

    before_step = {
        0: [lambda: column_in(3)],
        1: [lambda: column_whole(1), lambda: share(1)],
        2: [lambda: column_in(4), lambda: shared(1)],
        4: [lambda: share(2)],
        6: [lambda: shared(2)],
        8: [lambda: column_whole(2), lambda: share(3)],
        10: [lambda: shared(3)],
        12: [lambda: column_whole(3), lambda: share(4)],
        14: [lambda: shared(4)],
        16: [lambda: column_whole(4), lambda: share(5)],
        18: [lambda: shared(5)],
    }
    score(0)
    score(1)
    weigh(0)
    for i in range(len(work)):
        for event in before_step.get(i, ()):
            event()
        if i == len(work) - tiles:
            up_in.wait()
        mix(i)
        if i + 1 < len(work):
            weigh(i + 1)
        if i + 2 < len(work):
            score(i + 2)
        if i >= len(work) - tiles:
            finish(i - (len(work) - tiles))

    assert len(sent) == SENDS, len(sent)
    for when, copy in sent:
        pl.when(when)(copy.wait_send)
    everything = q.at[pl.ds(0, BACK * HALF)]
    pltpu.make_async_copy(everything, everything, core_send_sem.at[0]).wait()
    for copy in copies:
        copy.wait()


def local(queries, compressed_kv, segment_ids, value_up):
    any_space = pl.BlockSpec(memory_space=pl.ANY)
    return pl.pallas_call(
        kernel,
        out_shape=jax.ShapeDtypeStruct((TOK, HEADS * VDIM), bf16),
        in_specs=[any_space] * 5,
        out_specs=any_space,
        scratch_shapes=[
            pltpu.VMEM((BACK, TOK, WIDTH), bf16),
            pltpu.VMEM((ROWS, WIDTH), bf16),
            pltpu.VMEM((HEADS, LATENT + ROPE, TOK), bf16),
            pltpu.VMEM((QTR, LATENT + ROPE), bf16),
            pltpu.SMEM((QTR,), jnp.int32),
            pltpu.VMEM((ROPE, TOK), f32),
            pltpu.VMEM((TOK, ROPE), f32),
            pltpu.VMEM((ROWS, LATENT), f32),
            pltpu.VMEM((ROWS, TOK), f32),
            pltpu.VMEM((ROWS, TOK), f32),
            pltpu.VMEM((TILE, 4 * TOK), f32),
            pltpu.VMEM((TILE, 4 * TOK), f32),
            pltpu.VMEM((TILE, 4 * TOK), bf16),
            pltpu.VMEM((TILE, 4 * TOK), bf16),
            pltpu.VMEM((TILE, TOK), f32),
            pltpu.VMEM((TILE, TOK), f32),
            pltpu.VMEM((HEADS, LATENT, VDIM), bf16),
            pltpu.VMEM((TOK, HEADS * VDIM), bf16),
            pltpu.SemaphoreType.DMA((5,)),
            pltpu.SemaphoreType.DMA((4,)),
            pltpu.SemaphoreType.DMA((SENDS,)),
            pltpu.SemaphoreType.DMA((1,)),
            pltpu.SemaphoreType.DMA((5,)),
            pltpu.SemaphoreType.DMA((BACK,)),
            pltpu.SemaphoreType.DMA((BACK,)),
            pltpu.SemaphoreType.DMA((len(GROUPS),)),
        ],
        compiler_params=pltpu.CompilerParams(
            collective_id=0, has_side_effects=True, vmem_limit_bytes=62 << 20
        ),
        name="latent_attention",
    )(
        jnp.asarray(rope_table()),
        jnp.transpose(queries, (1, 2, 0)),
        compressed_kv,
        segment_ids,
        value_up,
    )


def solution(mesh):
    in_specs = (
        P("ctx", "head", None),
        P(("ctx", "head"), None),
        P(("ctx", "head")),
        P("head", None, None),
    )
    return jax.shard_map(
        local, mesh=mesh, in_specs=in_specs, out_specs=P("ctx", "head"), check_vma=False
    )
```
